1024 devices in a mesh: dom: 128 (over z, y), grp: 8 (over x, core).
Axes of the slice: x: 4, y: 4, z: 32, core: 2. Of those that a mesh axis runs over, the one named last changes fastest.
Arguments:
- features: bfloat16 [1048576, 256], P(('dom', 'grp')), may hold values from -6 to 6
- cotangent: bfloat16 [1048576, 256], P(('dom', 'grp')), may hold values from -6 to 6
- w_self: bfloat16 [256, 256], replicated, may hold values from -0.375 to 0.375
- w_nbr: bfloat16 [256, 256], replicated, may hold values from -0.375 to 0.375
- tile_vals: bfloat16 [1024, 40, 128, 128], P(('dom', 'grp')), may hold values from 0 to 0.2, as said below
- tile_dst: int32 [1024, 40], P(('dom', 'grp')), may hold values from 0 to 7, as said below
- tile_src: int32 [1024, 40], P(('dom', 'grp')), may hold values from 0 to 10, as said below
- tile_count: int32 [1024], P(('dom', 'grp')), may hold values from 10 to 40, as said below
- send_rows: int32 [1024, 256], P(('dom', 'grp')), may hold values from 0 to 1023
- hub_rows: int32 [1024, 16], P(('dom', 'grp')), may hold values from 0 to 1023, as said below
Outputs:
- activations: bfloat16 [1048576, 256], P(('dom', 'grp'))
- grad_features: bfloat16 [1048576, 256], P(('dom', 'grp'))
- grad_w_self: float32 [256, 256], replicated
- grad_w_nbr: float32 [256, 256], replicated
The draws below stay inside these ranges and needn't reach their ends.
Inputs may be any that keep to these rules, and one draw needn't show every extreme that they name: `tile_vals`: edge weights; slots from tile_count on are padding with stale values. A device's tiles name distinct pairs of tile_dst and tile_src. `tile_src`: blocks 0 to 7 are own rows, the next 2 boundary rows, the last 1 hub copies. `tile_count`: some device has all 40 slots live in every draw. `send_rows`: entries p * 2 to (p + 1) * 2 - 1 go to dom peer p; rows may repeat. `hub_rows`: distinct on each device.
All inputs are finite; a program needn't handle non-finite values.
Results may differ from the reference program's by a relative error of at most 0.0053.
Values may be sent and summed in bfloat16 or wider, within the bound.
No kernel may reach another device: no remote copies, remote signals or barrier semaphores. Data moves between devices by JAX's collectives and lax.ppermute only.
A program may use at most 64 MiB of HBM per device.

```python
import math
import jax
import jax.numpy as jnp
from jax import lax

D = 256
TILE = 128
NODE_DEV = 1024
HALO_DEV = 256
HUBS = 128
HALO_PEER = 2
HUB_DEV = 16
LOCAL_BLOCKS = 8
SOURCE_BLOCKS = 11
TILES_MAX = 40
NODES = 1048576
N_DOM = 128
N_GRP = 8


def tile_pairs(key):
    devices = N_DOM * N_GRP
    local_blocks = NODE_DEV // TILE
    source_blocks = (NODE_DEV + HALO_DEV + HUBS) // TILE
    sub_keys = jax.random.split(jax.random.fold_in(key, 11), devices)

    def single(sub_key):
        return jax.random.permutation(sub_key, local_blocks * source_blocks)[:TILES_MAX]
    pair_ids = jax.vmap(single)(sub_keys).astype(jnp.int32)
    return (pair_ids // source_blocks, pair_ids % source_blocks)


def draw_tile_dst(key, part):
    first_ids, second_ids = tile_pairs(key)
    return first_ids


def draw_tile_src(key, part):
    first_ids, second_ids = tile_pairs(key)
    return second_ids


def draw_tile_count(key, part):
    key = jax.random.fold_in(key, 5)
    devices = N_DOM * N_GRP
    key_base, key_heavy, key_pick, key_full = jax.random.split(key, 4)
    base_count = jax.random.randint(key_base, (devices,), TILES_MAX // 4, TILES_MAX // 2 + 1)
    heavy_count = jax.random.randint(key_heavy, (devices,), 3 * TILES_MAX // 4, TILES_MAX + 1)
    heavy_pick = jax.random.randint(key_pick, (devices,), 0, 8) == 0
    counts = jnp.where(heavy_pick, heavy_count, base_count)
    full_device = jax.random.randint(key_full, (), 0, devices)
    counts = counts.at[full_device].set(TILES_MAX)
    return counts.astype(jnp.int32)


def draw_tile_vals(key, part):
    key = jax.random.fold_in(key, 7)
    key_mask, key_value = jax.random.split(key, 2)
    tile_shape = (N_DOM * N_GRP, TILES_MAX, TILE, TILE)
    edge_mask = jax.random.bernoulli(key_mask, 1.0 / 16.0, tile_shape)
    edge_value = jax.random.uniform(key_value, tile_shape, jnp.float32, 0.02, 0.12)
    return jnp.where(edge_mask, edge_value, 0.0).astype(jnp.bfloat16)


def draw_hub_rows(key, part):
    key = jax.random.fold_in(key, 9)
    sub_keys = jax.random.split(key, N_DOM * N_GRP)

    def single(sub_key):
        return jax.random.permutation(sub_key, NODE_DEV)[:HUB_DEV]
    return jax.vmap(single)(sub_keys).astype(jnp.int32)


def place_ends(array, rng, smallest, top_value):
    longest = array.shape.index(max(array.shape))
    spots = []
    for shift in (0, 1):
        where = [jax.random.randint(jax.random.fold_in(rng, axis), (), 0, length) for axis, length in enumerate(array.shape)]
        where[longest] = (where[longest] + shift) % array.shape[longest]
        spots.append(tuple(where))
    return array.at[spots[0]].set(smallest).at[spots[1]].set(top_value)


def levels(own_key, shape, shards, low, largest):
    gain, own = 1.0, jax.random.fold_in(own_key, 6)
    for axis_at, shards_of in shards:
        draws = jnp.exp(jax.random.uniform(jax.random.fold_in(own, axis_at), (shards_of,), jnp.float32, low / len(shards), largest / len(shards)))
        gain = gain * jnp.repeat(draws, shape[axis_at] // shards_of).reshape([-1 if axis == axis_at else 1 for axis in range(len(shape))])
    return gain


def centred(own_key, extent, width, bound, shards=(), kind=jnp.bfloat16):
    values = width * jax.random.normal(own_key, extent, jnp.float32)
    if shards:
        values = values * levels(own_key, extent, shards, -0.22, 0.18)
    return jnp.clip(values, -bound, bound).astype(kind)


def setup_inputs(seed: int = 0) -> dict:
    keys = jax.random.split(jax.random.key(seed), 11)
    return {
        "features": centred(keys[0], (NODES, D), 1.0, 6.0, ((0, 1024),)),
        "cotangent": centred(keys[1], (NODES, D), 1.0, 6.0, ((0, 1024),)),
        "w_self": centred(keys[2], (D, D), D ** -0.5, 0.375),
        "w_nbr": centred(keys[3], (D, D), D ** -0.5, 0.375),
        "tile_vals": draw_tile_vals(jax.random.fold_in(keys[10], 71), 0),
        "tile_dst": draw_tile_dst(jax.random.fold_in(keys[10], 71), 0),
        "tile_src": draw_tile_src(jax.random.fold_in(keys[10], 71), 0),
        "tile_count": draw_tile_count(jax.random.fold_in(keys[10], 71), 0),
        "send_rows": place_ends(jax.random.randint(keys[8], (N_DOM * N_GRP, HALO_DEV), 0, NODE_DEV), jax.random.fold_in(keys[8], 1), 0, NODE_DEV - 1).astype(jnp.int32),
        "hub_rows": draw_hub_rows(jax.random.fold_in(keys[10], 71), 0),
    }


def pick_rows(row_block, indices):
    return row_block[indices]

def add_rows(base_rows, indices, values):
    return base_rows.at[indices].add(values)

def forward_tiles(inputs):
    source, tile_block, dst_ids, src_ids, live_mask = inputs
    gathered = source[src_ids]
    products = jnp.einsum('tij,tjd->tid', tile_block.astype(jnp.float32), gathered.astype(jnp.float32), precision=lax.Precision.HIGHEST)
    dst_onehot = (dst_ids[:, None] == jnp.arange(LOCAL_BLOCKS, dtype=jnp.int32)[None, :]).astype(jnp.float32) * live_mask[:, None]
    summed = jnp.einsum('tb,tid->bid', dst_onehot, products, precision=lax.Precision.HIGHEST)
    return summed.reshape(NODE_DEV, D).astype(jnp.bfloat16)

def backward_tiles(inputs):
    tile_block, dst_ids, src_ids, live_mask, agg_grad = inputs
    gathered = agg_grad.reshape(LOCAL_BLOCKS, TILE, D)[dst_ids]
    pieces = jnp.einsum('tij,tid->tjd', tile_block.astype(jnp.float32), gathered.astype(jnp.float32), precision=lax.Precision.HIGHEST)
    src_onehot = (src_ids[:, None] == jnp.arange(SOURCE_BLOCKS, dtype=jnp.int32)[None, :]).astype(jnp.float32) * live_mask[:, None]
    summed = jnp.einsum('ts,tjd->sjd', src_onehot, pieces, precision=lax.Precision.HIGHEST)
    return summed.reshape(SOURCE_BLOCKS * TILE, D)

def reference(features, cotangent, w_self, w_nbr, tile_vals, tile_dst, tile_src, tile_count, send_rows, hub_rows):
    devices = N_DOM * N_GRP
    own_rows = features.reshape(N_DOM, N_GRP, NODE_DEV, D)
    send_lists = send_rows.reshape(N_DOM, N_GRP, N_DOM, HALO_PEER)
    sent_rows = jax.vmap(jax.vmap(pick_rows))(own_rows, send_lists)
    boundary = jnp.transpose(sent_rows, (2, 1, 0, 3, 4)).reshape(N_DOM, N_GRP, HALO_DEV, D)
    hub_lists = hub_rows.reshape(N_DOM, N_GRP, HUB_DEV)
    hub_picked = jax.vmap(jax.vmap(pick_rows))(own_rows, hub_lists)
    hub_copies = jnp.broadcast_to(hub_picked.reshape(N_DOM, 1, HUBS, D), (N_DOM, N_GRP, HUBS, D))
    source = jnp.concatenate([own_rows, boundary, hub_copies], axis=2).reshape(devices, SOURCE_BLOCKS, TILE, D)
    live_mask = (jnp.arange(TILES_MAX, dtype=jnp.int32)[None, :] < tile_count[:, None]).astype(jnp.float32)
    aggregated = lax.map(forward_tiles, (source, tile_vals, tile_dst, tile_src, live_mask)).reshape(NODES, D)
    pre = jnp.dot(features, w_self, preferred_element_type=jnp.float32) + jnp.dot(aggregated, w_nbr, preferred_element_type=jnp.float32)
    sigmoid_pre = jax.nn.sigmoid(pre)
    activations = (pre * sigmoid_pre).astype(jnp.bfloat16)
    pre_grad = (cotangent.astype(jnp.float32) * sigmoid_pre * (1.0 + pre * (1.0 - sigmoid_pre))).astype(jnp.bfloat16)
    contract_last = (((1,), (1,)), ((), ()))
    self_grad = lax.dot_general(pre_grad, w_self, contract_last, preferred_element_type=jnp.float32)
    agg_grad = lax.dot_general(pre_grad, w_nbr, contract_last, preferred_element_type=jnp.float32).astype(jnp.bfloat16)
    source_grad = lax.map(backward_tiles, (tile_vals, tile_dst, tile_src, live_mask, agg_grad.reshape(devices, NODE_DEV, D)))
    local_grad = source_grad[:, :NODE_DEV]
    boundary_grad = source_grad[:, NODE_DEV:NODE_DEV + HALO_DEV].astype(jnp.bfloat16)
    boundary_grad = boundary_grad.reshape(N_DOM, N_GRP, N_DOM, HALO_PEER, D)
    returned = jnp.transpose(boundary_grad, (2, 1, 0, 3, 4)).reshape(devices, HALO_DEV, D)
    hub_grad = source_grad[:, NODE_DEV + HALO_DEV:].reshape(N_DOM, N_GRP, HUBS, D).sum(axis=1)
    hub_grad = hub_grad.reshape(devices, HUB_DEV, D)
    summed = self_grad.reshape(devices, NODE_DEV, D) + local_grad
    summed = jax.vmap(add_rows)(summed, send_rows, returned.astype(jnp.float32))
    summed = jax.vmap(add_rows)(summed, hub_rows, hub_grad)
    grad_features = summed.reshape(NODES, D).astype(jnp.bfloat16)
    grad_scale = 1.0 / math.sqrt(NODES)
    contract_rows = (((0,), (0,)), ((), ()))
    grad_w_self = lax.dot_general(features, pre_grad, contract_rows, preferred_element_type=jnp.float32) * grad_scale
    grad_w_nbr = lax.dot_general(aggregated, pre_grad, contract_rows, preferred_element_type=jnp.float32) * grad_scale
    return (activations, grad_features, grad_w_self, grad_w_nbr)
```

```python
import math

import jax
import jax.numpy as jnp
from jax import lax
from jax.experimental import pallas as pl
from jax.experimental.pallas import tpu as pltpu
from jax.sharding import Mesh
from jax.sharding import PartitionSpec as P

TILE = 128
ROWS = 1024
HALO = 256
HUBS = 128
HUB_DEV = 16
PART = 64
LOAD = PART + HUB_DEV
LOCAL = 8
SOURCE = 11
TILES = 40
D = 256
CHUNK = 256
AXES = ("zh", "zl", "y", "x", "c")
ZL = 8
ZH = 4
BF16 = jnp.bfloat16
F32 = jnp.float32
VMEM_LIMIT = 60 * 1024 * 1024
SMALL_LIMIT = 16 * 1024 * 1024

VM = pl.BlockSpec(memory_space=pltpu.VMEM)
ANY = pl.BlockSpec(memory_space=pl.ANY)
SM = pl.BlockSpec(memory_space=pltpu.SMEM)


def dot(a, b):
    return jnp.dot(a, b, preferred_element_type=F32)


def call(kernel, outs, specs, scratch=(), flops=0, nbytes=0, trans=0, limit=VMEM_LIMIT):
    return pl.pallas_call(
        kernel,
        out_shape=[jax.ShapeDtypeStruct(s, t) for s, t in outs],
        in_specs=list(specs),
        out_specs=[VM] * len(outs),
        scratch_shapes=list(scratch),
        compiler_params=pltpu.CompilerParams(vmem_limit_bytes=limit),
        cost_estimate=pl.CostEstimate(flops=flops, bytes_accessed=nbytes, transcendentals=trans),
    )


def column_of(row, count):
    here = lax.broadcasted_iota(jnp.int32, (count, count), 0)
    there = lax.broadcasted_iota(jnp.int32, (count, count), 1)
    spread = jnp.where(here == there, jnp.broadcast_to(row, (count, count)).astype(F32), 0.0)
    return jnp.sum(spread, axis=1, keepdims=True).astype(jnp.int32)


def pick_kernel(send_ref, hub_ref, x_ref, sent_ref, hubs_ref):
    for idx_ref, out_ref in ((hub_ref, hubs_ref), (send_ref, sent_ref)):
        count = out_ref.shape[0]
        column = column_of(idx_ref[...], count)
        lanes = lax.broadcasted_iota(jnp.int32, (count, ROWS), 1)
        onehot = jnp.where(lanes == column, 1.0, 0.0).astype(BF16)
        out_ref[...] = dot(onehot, x_ref[...]).astype(BF16)


def prep_kernel(
    count_ref, dst_ref, src_ref, tiles_ref, x_ref, ws_ref, wn_ref,
    rem_ref, at_ref, part_ref, self_ref, xt_ref, wst_ref, wnt_ref, a_ref,
):
    a_ref[...] = jnp.zeros_like(a_ref)
    at_ref[...] = jnp.zeros_like(at_ref)

    def place(t, carry):
        tile = tiles_ref[0, t]
        row = pl.multiple_of(dst_ref[0, t] * TILE, TILE)
        col = pl.multiple_of(src_ref[0, t] * TILE, TILE)
        a_ref[pl.ds(row, TILE), pl.ds(col, TILE)] = tile
        at_ref[pl.ds(col, TILE), pl.ds(row, TILE)] = tile.T
        return carry

    lax.fori_loop(0, count_ref[0], place, 0)
    rem_ref[...] = a_ref[:, ROWS:]
    wst_ref[...] = ws_ref[...].T
    wnt_ref[...] = wn_ref[...].T
    for i in range(ROWS // CHUNK):
        rows = slice(i * CHUNK, (i + 1) * CHUNK)
        part_ref[rows, :] = dot(a_ref[rows, :ROWS], x_ref[...])
        self_ref[rows, :] = dot(x_ref[rows, :], ws_ref[...])
        xt_ref[:, rows] = x_ref[rows, :].T


def middle_kernel(
    rem_ref, atrem_ref, bnd_ref, hub_ref, part_ref, self_ref, cot_ref, xt_ref, wn_ref, wnt_ref,
    act_ref, pg_ref, ag_ref, bg_ref, load_ref,
):
    scale = 1.0 / math.sqrt(1048576)
    gself = jnp.zeros((D, D), F32)
    gnbr = jnp.zeros((D, D), F32)
    for i in range(ROWS // CHUNK):
        rows = slice(i * CHUNK, (i + 1) * CHUNK)
        agg = (
            part_ref[rows, :]
            + dot(rem_ref[rows, :HALO], bnd_ref[...])
            + dot(rem_ref[rows, HALO:], hub_ref[...])
        ).astype(BF16)
        pre = self_ref[rows, :] + dot(agg, wn_ref[...])
        sig = jax.nn.sigmoid(pre)
        act_ref[rows, :] = (pre * sig).astype(BF16)
        pg = (cot_ref[rows, :].astype(F32) * sig * (1.0 + pre * (1.0 - sig))).astype(BF16)
        pg_ref[rows, :] = pg
        ag_ref[rows, :] = dot(pg, wnt_ref[...]).astype(BF16)
        gself = gself + dot(xt_ref[:, rows], pg)
        gnbr = gnbr + lax.dot_general(agg, pg, (((0,), (0,)), ((), ())), preferred_element_type=F32)
    bg_ref[...] = dot(atrem_ref[:HALO, :], ag_ref[...]).astype(BF16)
    hub_grad = dot(atrem_ref[HALO:, :], ag_ref[...])
    for k in range(8):
        at = k * LOAD
        grad = (gself, gnbr)[k // 4][(k % 4) * PART : (k % 4 + 1) * PART, :]
        load_ref[at : at + PART, :] = grad * scale
        load_ref[at + PART : at + LOAD, :] = hub_grad[k * HUB_DEV : (k + 1) * HUB_DEV, :]


def split_kernel(in_ref, grad_ref, hub_ref):
    total = in_ref[:LOAD, :]
    for k in range(1, 8):
        total = total + in_ref[k * LOAD : (k + 1) * LOAD, :]
    grad_ref[...] = total[:PART, :]
    hub_ref[...] = total[PART:, :]


def sum_kernel(parts, copies):
    def kernel(in_ref, *refs):
        out_ref = refs[-1]
        height = in_ref.shape[0] // parts
        total = in_ref[:height, :]
        for p in range(1, parts):
            total = total + in_ref[p * height : (p + 1) * height, :]
        total = total.astype(out_ref.dtype)
        for q in range(copies):
            out_ref[q * height : (q + 1) * height, :] = total

    return kernel


def final_kernel(send_ref, hub_ref, ret_ref, hsum_ref, pg_ref, ag_ref, wst_ref, at_ref, out_ref):
    ret = ret_ref[...]
    high = hsum_ref[...].astype(BF16)
    low = (hsum_ref[...] - high.astype(F32)).astype(BF16)
    for i in range(ROWS // CHUNK):
        rows = slice(i * CHUNK, (i + 1) * CHUNK)
        total = dot(pg_ref[rows, :], wst_ref[...]) + dot(at_ref[rows, :], ag_ref[...])
        own = lax.broadcasted_iota(jnp.int32, (CHUNK, HALO), 0) + i * CHUNK
        total = total + dot(jnp.where(own == send_ref[...], 1.0, 0.0).astype(BF16), ret)
        own = lax.broadcasted_iota(jnp.int32, (CHUNK, HUB_DEV), 0) + i * CHUNK
        hub_hot = jnp.where(own == hub_ref[...], 1.0, 0.0).astype(BF16)
        total = total + dot(hub_hot, high) + dot(hub_hot, low)
        out_ref[rows, :] = total.astype(BF16)


def per_device(
    features, cotangent, w_self, w_nbr, tile_vals, tile_dst, tile_src, tile_count, send_rows, hub_rows
):
    mib = 1 << 20
    dom = ("zh", "zl", "y")
    grp = ("x", "c")
    sent, hubs = call(
        pick_kernel, [((HALO, D), BF16), ((HUB_DEV, D), BF16)], [VM] * 3, flops=1 << 28, nbytes=mib
    )(send_rows, hub_rows, features)
    boundary = lax.all_to_all(sent, dom, 0, 0, tiled=True)
    hub_copies = lax.all_gather(hubs, grp, axis=0, tiled=True)
    rem, at, part, self_pre, xt, wst, wnt = call(
        prep_kernel,
        [
            ((ROWS, HALO + HUBS), BF16),
            ((SOURCE * TILE, ROWS), BF16),
            ((ROWS, D), F32),
            ((ROWS, D), F32),
            ((D, ROWS), BF16),
            ((D, D), BF16),
            ((D, D), BF16),
        ],
        [SM, SM, SM, VM, VM, VM, VM],
        scratch=[pltpu.VMEM((ROWS, SOURCE * TILE), BF16)],
        flops=1 << 30,
        nbytes=9 * mib,
    )(tile_count, tile_dst, tile_src, tile_vals, features, w_self, w_nbr)
    at_rem = at[ROWS:]
    act, pg, ag, bg, load = call(
        middle_kernel,
        [
            ((ROWS, D), BF16),
            ((ROWS, D), BF16),
            ((ROWS, D), BF16),
            ((HALO, D), BF16),
            ((8 * LOAD, D), F32),
        ],
        [VM] * 10,
        flops=1 << 30,
        nbytes=8 * mib,
        trans=1 << 19,
    )(rem, at_rem, boundary, hub_copies, part, self_pre, cotangent, xt, w_nbr, wnt)

    height = 2 * D // 32
    load = lax.all_to_all(load, grp, 0, 0, tiled=True)
    part, hub_sums = call(
        split_kernel, [((PART, D), F32), ((HUB_DEV, D), F32)], [VM], nbytes=mib, limit=SMALL_LIMIT
    )(load)
    part = lax.all_to_all(part, "y", 0, 0, tiled=True)
    (chunk,) = call(sum_kernel(4, 1), [((height, D), F32)], [VM], limit=SMALL_LIMIT)(part)
    bg, chunk = lax.optimization_barrier((bg.reshape(HALO // 2, 2, D), chunk))
    returned = lax.all_to_all(bg, dom, 0, 0, tiled=True).reshape(HALO, D)
    for bit in (1, 2, 4):
        chunk = chunk + lax.ppermute(chunk, "zl", [(i, i ^ bit) for i in range(ZL)])
    (chunk,) = call(sum_kernel(1, ZH), [((height * ZH, D), F32)], [VM, ANY], limit=SMALL_LIMIT)(
        chunk, returned
    )
    chunk = lax.all_to_all(chunk, "zh", 0, 0, tiled=True)
    (chunk,) = call(sum_kernel(ZH, 32), [((2 * D, D), BF16)], [VM], limit=SMALL_LIMIT)(chunk)
    grads = lax.all_to_all(chunk, ("x", "c", "y"), 0, 0, tiled=True)
    (grad_features,) = call(
        final_kernel, [((ROWS, D), BF16)], [VM] * 8, flops=1 << 30, nbytes=6 * mib
    )(send_rows, hub_rows, returned, hub_sums, pg, ag, wst, at)
    grads = grads.astype(F32)
    return act, grad_features, grads[:D], grads[D:]


def solution(mesh):
    fine = Mesh(mesh.devices.reshape(ZH, ZL, 4, 4, 2), AXES)
    whole = P(AXES, None)
    return jax.shard_map(
        per_device,
        mesh=fine,
        in_specs=(
            whole,
            whole,
            P(),
            P(),
            P(AXES, None, None, None),
            whole,
            whole,
            P(AXES),
            whole,
            whole,
        ),
        out_specs=(whole, whole, P(), P()),
        check_vma=False,
    )
```

```python
import math

import jax
import jax.numpy as jnp
import numpy as np
from jax import lax
from jax.experimental import pallas as pl
from jax.experimental.pallas import tpu as pltpu
from jax.sharding import Mesh
from jax.sharding import PartitionSpec as P

TILE = 128
ROWS = 1024
HALO = 256
HUBS = 128
HUB_DEV = 16
PART = 128
HALF = 128
LOAD = PART + 2 * HUB_DEV
LOCAL = 8
SOURCE = 11
TILES = 40
D = 256
PACK = D + HALF
TURN = HALO // 2
CHUNK = 256
ZL = 4
ZH = 8
NEAR = 16
FAR = 40
ALONG = np.arange(1024).reshape(ZH, ZL, 4, 4, 2)


def groups(order, turn=0):
    others = [axis for axis in range(5) if axis not in order]
    table = ALONG.transpose(others + list(order))
    table = np.roll(table, -turn, axis=len(others))
    return table.reshape(-1, math.prod(ALONG.shape[axis] for axis in order)).tolist()


def swap_rows(array, order, turn=0):
    return lax.all_to_all(array, "d", 0, 0, axis_index_groups=groups(order, turn), tiled=True)


BF16 = jnp.bfloat16
F32 = jnp.float32
VMEM_LIMIT = 60 * 1024 * 1024
SMALL_LIMIT = 16 * 1024 * 1024

VM = pl.BlockSpec(memory_space=pltpu.VMEM)
SM = pl.BlockSpec(memory_space=pltpu.SMEM)


def dot(a, b):
    return jnp.dot(a, b, preferred_element_type=F32)


def call(kernel, outs, specs, scratch=(), flops=0, nbytes=0, trans=0, limit=VMEM_LIMIT):
    return pl.pallas_call(
        kernel,
        out_shape=[jax.ShapeDtypeStruct(s, t) for s, t in outs],
        in_specs=list(specs),
        out_specs=[VM] * len(outs),
        scratch_shapes=list(scratch),
        compiler_params=pltpu.CompilerParams(vmem_limit_bytes=limit),
        cost_estimate=pl.CostEstimate(flops=flops, bytes_accessed=nbytes, transcendentals=trans),
    )


def column_of(row, count):
    here = lax.broadcasted_iota(jnp.int32, (count, count), 0)
    there = lax.broadcasted_iota(jnp.int32, (count, count), 1)
    spread = jnp.where(here == there, jnp.broadcast_to(row, (count, count)).astype(F32), 0.0)
    return jnp.sum(spread, axis=1, keepdims=True).astype(jnp.int32)


def permute(first, second, turn=0):
    to = lax.broadcasted_iota(jnp.int32, (HALO, HALO), 0)
    at = lax.broadcasted_iota(jnp.int32, (HALO, HALO), 1)
    inner, pair = to // 2 % first, (to // (2 * first) + turn) % second
    return jnp.where(at == (inner * second + pair) * 2 + to % 2, 1.0, 0.0).astype(BF16)


def halves(value):
    high = value.astype(BF16).astype(F32)
    return jnp.concatenate([high, value - high], axis=0).astype(BF16)


def pick_kernel(send_ref, hub_ref, x_ref, sent_ref, hubs_ref):
    def picked(idx_ref):
        count = idx_ref.shape[1]
        column = column_of(idx_ref[...], count)
        lanes = lax.broadcasted_iota(jnp.int32, (count, ROWS), 1)
        onehot = jnp.where(lanes == column, 1.0, 0.0).astype(BF16)
        return dot(onehot, x_ref[...]).astype(BF16)

    sent = picked(send_ref)
    sent_ref[:TURN, :] = sent[TURN:, :]
    sent_ref[TURN:, :] = sent[:TURN, :]
    hubs_ref[...] = picked(hub_ref)


def prep_kernel(
    count_ref, dst_ref, src_ref, tiles_ref, x_ref, ws_ref, wn_ref,
    rem_ref, atrem_ref, part_ref, self_ref, xt_ref, wnt_ref, a_ref, far_ref,
):
    a_ref[...] = jnp.zeros_like(a_ref)
    far_ref[...] = jnp.zeros_like(far_ref)

    def place(t, carry):
        row = pl.multiple_of(dst_ref[0, t] * TILE, TILE)
        source = src_ref[0, t]
        a_ref[pl.ds(row, TILE), pl.ds(pl.multiple_of(source * TILE, TILE), TILE)] = tiles_ref[0, t]

        @pl.when(source >= LOCAL)
        def _():
            col = pl.multiple_of((source - LOCAL) * TILE, TILE)
            far_ref[pl.ds(col, TILE), pl.ds(row, TILE)] = tiles_ref[0, t].T

        return carry

    lax.fori_loop(0, count_ref[0], place, 0)
    rem_ref[:, :TURN] = a_ref[:, ROWS + TURN : ROWS + HALO]
    rem_ref[:, TURN:HALO] = a_ref[:, ROWS : ROWS + TURN]
    rem_ref[:, HALO:] = a_ref[:, ROWS + HALO :]
    atrem_ref[:HALO, :] = dot(permute(ZH, NEAR), far_ref[:HALO, :]).astype(BF16)
    atrem_ref[HALO:, :] = far_ref[HALO:, :]
    wnt_ref[...] = wn_ref[...].T
    for i in range(ROWS // CHUNK):
        rows = slice(i * CHUNK, (i + 1) * CHUNK)
        part_ref[rows, :] = dot(a_ref[rows, :ROWS], x_ref[...])
        self_ref[rows, :] = dot(x_ref[rows, :], ws_ref[...])
        xt_ref[:, rows] = x_ref[rows, :].T


def middle_kernel(
    rem_ref, atrem_ref, bnd_ref, hub_ref, part_ref, self_ref, cot_ref, xt_ref, wn_ref, wnt_ref,
    act_ref, pg_ref, ag_ref, bg_ref, load_ref,
):
    scale = 1.0 / math.sqrt(1048576)
    gself = jnp.zeros((D, D), F32)
    gnbr = jnp.zeros((D, D), F32)
    for i in range(ROWS // CHUNK):
        rows = slice(i * CHUNK, (i + 1) * CHUNK)
        agg = (
            part_ref[rows, :]
            + dot(rem_ref[rows, :HALO], bnd_ref[...])
            + dot(rem_ref[rows, HALO:], hub_ref[...])
        ).astype(BF16)
        pre = self_ref[rows, :] + dot(agg, wn_ref[...])
        sig = jax.nn.sigmoid(pre)
        act_ref[rows, :] = (pre * sig).astype(BF16)
        pg = (cot_ref[rows, :].astype(F32) * sig * (1.0 + pre * (1.0 - sig))).astype(BF16)
        pg_ref[rows, :] = pg
        ag_ref[rows, :] = dot(pg, wnt_ref[...]).astype(BF16)
        gself = gself + dot(xt_ref[:, rows], pg)
        gnbr = gnbr + lax.dot_general(agg, pg, (((0,), (0,)), ((), ())), preferred_element_type=F32)
    bg_ref[...] = dot(atrem_ref[:HALO, :], ag_ref[...]).astype(BF16)
    hub_grad = dot(atrem_ref[HALO:, :], ag_ref[...])
    for k in range(8):
        lanes = slice(k // 4 * HALF, (k // 4 + 1) * HALF)
        rows = slice(k % 2 * PART, (k % 2 + 1) * PART)
        at = k * LOAD
        load_ref[at : at + PART, :] = (gself, gnbr)[k // 2 % 2][rows, lanes] * scale
        hub = hub_grad[k * HUB_DEV : (k + 1) * HUB_DEV, :]
        load_ref[at + PART : at + PART + HUB_DEV, :] = hub[:, :HALF]
        load_ref[at + PART + HUB_DEV : at + LOAD, :] = hub[:, HALF:]


def near_kernel(in_ref, bg_ref, out_ref, hub_ref):
    total = in_ref[:LOAD, :]
    for k in range(1, 8):
        total = total + in_ref[k * LOAD : (k + 1) * LOAD, :]
    hub_ref[:, :HALF] = total[PART : PART + HUB_DEV, :]
    hub_ref[:, HALF:] = total[PART + HUB_DEV :, :]
    out_ref[:, :D] = bg_ref[...]
    for m in range(NEAR):
        out_ref[m * 16 : (m + 1) * 16, D:] = halves(total[m * 8 : (m + 1) * 8, :])


def far_kernel(in_ref, out_ref):
    total = in_ref[:16, D:].astype(F32)
    for m in range(1, NEAR):
        total = total + in_ref[m * 16 : (m + 1) * 16, D:].astype(F32)
    chunk = total[:8, :] + total[8:, :]
    high = chunk.astype(BF16).astype(F32)
    both = jnp.concatenate([high, chunk - high], axis=1)
    moved = dot(permute(NEAR, ZH, ZH // 2), in_ref[:, :D])
    for j in range(ZH // 2):
        block = [moved[j * 64 : j * 64 + 32, :], both, moved[j * 64 + 32 : j * 64 + 64, :], both]
        out_ref[j * 2 * FAR : (j + 1) * 2 * FAR, :] = jnp.concatenate(block, axis=0).astype(BF16)


def far_blocks(in_ref):
    for j in range(ZH // 2):
        block = in_ref[j * 2 * FAR : (j + 1) * 2 * FAR, :].astype(F32)
        yield block[:FAR, :]
        yield block[FAR:, :]


def spread_kernel(in_ref, out_ref):
    total = jnp.zeros((8, D), F32)
    for block in far_blocks(in_ref):
        total = total + block[32:, :]
    chunk = total[:, :HALF] + total[:, HALF:]
    both = jnp.concatenate([chunk, chunk], axis=0).astype(BF16)
    for q in range(out_ref.shape[0] // 16):
        out_ref[q * 16 : (q + 1) * 16, :] = both


def final_kernel(
    count_ref, dst_ref, src_ref, send_ref, hub_ref, ret_ref, hsum_ref, pg_ref, ag_ref, ws_ref, tiles_ref,
    out_ref, at_ref,
):
    at_ref[...] = jnp.zeros_like(at_ref)

    def place(t, carry):
        source = src_ref[0, t]

        @pl.when(source < LOCAL)
        def _():
            row = pl.multiple_of(source * TILE, TILE)
            col = pl.multiple_of(dst_ref[0, t] * TILE, TILE)
            at_ref[pl.ds(row, TILE), pl.ds(col, TILE)] = tiles_ref[0, t].T

        return carry

    lax.fori_loop(0, count_ref[0], place, 0)
    blocks = [block[:32, :] for block in far_blocks(ret_ref)]
    ret = jnp.concatenate(blocks[ZH // 2 :] + blocks[: ZH // 2], axis=0).astype(BF16)
    high = hsum_ref[...].astype(BF16)
    low = (hsum_ref[...] - high.astype(F32)).astype(BF16)
    wst = ws_ref[...].T
    for i in range(ROWS // CHUNK):
        rows = slice(i * CHUNK, (i + 1) * CHUNK)
        total = dot(pg_ref[rows, :], wst) + dot(at_ref[rows, :], ag_ref[...])
        own = lax.broadcasted_iota(jnp.int32, (CHUNK, HALO), 0) + i * CHUNK
        total = total + dot(jnp.where(own == send_ref[...], 1.0, 0.0).astype(BF16), ret)
        own = lax.broadcasted_iota(jnp.int32, (CHUNK, HUB_DEV), 0) + i * CHUNK
        hub_hot = jnp.where(own == hub_ref[...], 1.0, 0.0).astype(BF16)
        total = total + dot(hub_hot, high) + dot(hub_hot, low)
        out_ref[rows, :] = total.astype(BF16)


def per_device(
    features, cotangent, w_self, w_nbr, tile_vals, tile_dst, tile_src, tile_count, send_rows, hub_rows
):
    mib = 1 << 20
    sent, hubs = call(
        pick_kernel, [((HALO, D), BF16), ((HUB_DEV, D), BF16)], [VM] * 3, flops=1 << 28, nbytes=mib
    )(send_rows, hub_rows, features)
    boundary = swap_rows(sent, (0, 1, 2), ZH // 2)
    hub_copies = hubs
    for axis in (4, 3):
        hub_copies = lax.all_gather(hub_copies, "d", axis_index_groups=groups((axis,)), axis=0, tiled=True)
    rem, at_rem, part, self_pre, xt, wnt = call(
        prep_kernel,
        [
            ((ROWS, HALO + HUBS), BF16),
            ((HALO + HUBS, ROWS), BF16),
            ((ROWS, D), F32),
            ((ROWS, D), F32),
            ((D, ROWS), BF16),
            ((D, D), BF16),
        ],
        [SM, SM, SM, VM, VM, VM, VM],
        scratch=[pltpu.VMEM((ROWS, SOURCE * TILE), BF16), pltpu.VMEM((HALO + HUBS, ROWS), BF16)],
        flops=1 << 30,
        nbytes=9 * mib,
    )(tile_count, tile_dst, tile_src, tile_vals, features, w_self, w_nbr)
    act, pg, ag, bg, load = call(
        middle_kernel,
        [
            ((ROWS, D), BF16),
            ((ROWS, D), BF16),
            ((ROWS, D), BF16),
            ((HALO, D), BF16),
            ((8 * LOAD, HALF), F32),
        ],
        [VM] * 10,
        flops=1 << 30,
        nbytes=8 * mib,
        trans=1 << 19,
    )(rem, at_rem, boundary, hub_copies, part, self_pre, cotangent, xt, w_nbr, wnt)

    load = swap_rows(load, (3, 4))
    near, hub_sums = call(
        near_kernel, [((HALO, PACK), BF16), ((HUB_DEV, D), F32)], [VM] * 2, nbytes=mib, limit=SMALL_LIMIT
    )(load, bg)
    near = swap_rows(near, (1, 2))
    (far,) = call(far_kernel, [((ZH * FAR, D), BF16)], [VM], nbytes=mib, limit=SMALL_LIMIT)(near)
    returned = swap_rows(far, (0,), ZH // 2)
    (chunk,) = call(spread_kernel, [((4 * D, HALF), BF16)], [VM], nbytes=mib, limit=SMALL_LIMIT)(returned)
    grads = swap_rows(chunk, (3, 4, 1, 2))
    (grad_features,) = call(
        final_kernel,
        [((ROWS, D), BF16)],
        [SM] * 3 + [VM] * 8,
        scratch=[pltpu.VMEM((ROWS, ROWS), BF16)],
        flops=1 << 30,
        nbytes=5 * mib,
    )(tile_count, tile_dst, tile_src, send_rows, hub_rows, returned, hub_sums, pg, ag, w_self, tile_vals)
    grads = grads.astype(F32).reshape(2, 2, D, HALF)
    grads = jnp.concatenate([grads[0], grads[1]], axis=2)
    return act, grad_features, grads[0], grads[1]


def solution(mesh):
    whole = P("d", None)
    return jax.shard_map(
        per_device,
        mesh=Mesh(mesh.devices.reshape(-1), ("d",)),
        in_specs=(
            whole,
            whole,
            P(),
            P(),
            P("d", None, None, None),
            whole,
            whole,
            P("d"),
            whole,
            whole,
        ),
        out_specs=(whole, whole, P(), P()),
        check_vma=False,
    )
```

```python
import math

import jax
import jax.numpy as jnp
import numpy as np
from jax import lax
from jax.experimental import pallas as pl
from jax.experimental.pallas import tpu as pltpu
from jax.sharding import Mesh
from jax.sharding import PartitionSpec as P

TILE = 128
ROWS = 1024
HALO = 256
HUBS = 128
HUB_DEV = 16
PART = 128
HALF = 128
LOAD = PART + 2 * HUB_DEV
LOCAL = 8
SOURCE = 11
TILES = 40
D = 256
PACK = D + HALF
TURN = HALO // 2
CHUNK = 256
ZL = 4
ZH = 8
NEAR = 16
FAR = 40
ALONG = np.arange(1024).reshape(ZH, ZL, 4, 4, 2)


def groups(order, turn=0):
    others = [axis for axis in range(5) if axis not in order]
    table = ALONG.transpose(others + list(order))
    table = np.roll(table, -turn, axis=len(others))
    return table.reshape(-1, math.prod(ALONG.shape[axis] for axis in order)).tolist()


def swap_rows(array, order, turn=0):
    return lax.all_to_all(array, "d", 0, 0, axis_index_groups=groups(order, turn), tiled=True)


BF16 = jnp.bfloat16
F32 = jnp.float32
VMEM_LIMIT = 60 * 1024 * 1024
SMALL_LIMIT = 16 * 1024 * 1024

VM = pl.BlockSpec(memory_space=pltpu.VMEM)
SM = pl.BlockSpec(memory_space=pltpu.SMEM)


def dot(a, b):
    return jnp.dot(a, b, preferred_element_type=F32)


def call(kernel, outs, specs, scratch=(), flops=0, nbytes=0, trans=0, limit=VMEM_LIMIT):
    return pl.pallas_call(
        kernel,
        out_shape=[jax.ShapeDtypeStruct(s, t) for s, t in outs],
        in_specs=list(specs),
        out_specs=[VM] * len(outs),
        scratch_shapes=list(scratch),
        compiler_params=pltpu.CompilerParams(vmem_limit_bytes=limit),
        cost_estimate=pl.CostEstimate(flops=flops, bytes_accessed=nbytes, transcendentals=trans),
    )


def column_of(row, count):
    here = lax.broadcasted_iota(jnp.int32, (count, count), 0)
    there = lax.broadcasted_iota(jnp.int32, (count, count), 1)
    spread = jnp.where(here == there, jnp.broadcast_to(row, (count, count)).astype(F32), 0.0)
    return jnp.sum(spread, axis=1, keepdims=True).astype(jnp.int32)


def permute(first, second, turn=0):
    to = lax.broadcasted_iota(jnp.int32, (HALO, HALO), 0)
    at = lax.broadcasted_iota(jnp.int32, (HALO, HALO), 1)
    inner, pair = to // 2 % first, (to // (2 * first) + turn) % second
    return jnp.where(at == (inner * second + pair) * 2 + to % 2, 1.0, 0.0).astype(BF16)


def halves(value):
    high = value.astype(BF16).astype(F32)
    return jnp.concatenate([high, value - high], axis=0).astype(BF16)


def pick_kernel(send_ref, hub_ref, x_ref, sent_ref, hubs_ref):
    def picked(idx_ref):
        count = idx_ref.shape[1]
        column = column_of(idx_ref[...], count)
        lanes = lax.broadcasted_iota(jnp.int32, (count, ROWS), 1)
        onehot = jnp.where(lanes == column, 1.0, 0.0).astype(BF16)
        return dot(onehot, x_ref[...])

    sent = picked(send_ref)
    sent = jnp.concatenate([sent[TURN:, :], sent[:TURN, :]], axis=0)
    sent_ref[...] = sent.reshape(sent_ref.shape).astype(BF16)
    hubs_ref[...] = picked(hub_ref).astype(BF16)


def prep_kernel(
    count_ref, dst_ref, src_ref, tiles_ref, x_ref, ws_ref, wn_ref,
    rem_ref, atrem_ref, part_ref, self_ref, xt_ref, wnt_ref, a_ref, far_ref,
):
    a_ref[...] = jnp.zeros_like(a_ref)
    far_ref[...] = jnp.zeros_like(far_ref)

    def place(t, carry):
        row = pl.multiple_of(dst_ref[0, t] * TILE, TILE)
        source = src_ref[0, t]
        a_ref[pl.ds(row, TILE), pl.ds(pl.multiple_of(source * TILE, TILE), TILE)] = tiles_ref[0, t]

        @pl.when(source >= LOCAL)
        def _():
            col = pl.multiple_of((source - LOCAL) * TILE, TILE)
            far_ref[pl.ds(col, TILE), pl.ds(row, TILE)] = tiles_ref[0, t].T

        return carry

    lax.fori_loop(0, count_ref[0], place, 0)
    rem_ref[:, :TURN] = a_ref[:, ROWS + TURN : ROWS + HALO]
    rem_ref[:, TURN:HALO] = a_ref[:, ROWS : ROWS + TURN]
    rem_ref[:, HALO:] = a_ref[:, ROWS + HALO :]
    atrem_ref[:HALO, :] = dot(permute(ZH, NEAR), far_ref[:HALO, :]).astype(BF16)
    atrem_ref[HALO:, :] = far_ref[HALO:, :]
    wnt_ref[...] = wn_ref[...].T
    for i in range(ROWS // CHUNK):
        rows = slice(i * CHUNK, (i + 1) * CHUNK)
        part_ref[rows, :] = dot(a_ref[rows, :ROWS], x_ref[...])
        self_ref[rows, :] = dot(x_ref[rows, :], ws_ref[...])
        xt_ref[:, rows] = x_ref[rows, :].T


def middle_kernel(
    rem_ref, atrem_ref, bnd_ref, hub0_ref, hub1_ref, hub2_ref, hub3_ref, part_ref, self_ref, cot_ref, xt_ref, wn_ref, wnt_ref,
    act_ref, pg_ref, ag_ref, bg_ref, load_ref, hub_ref,
):
    scale = 1.0 / math.sqrt(1048576)
    here = lax.axis_index("d") // 2 % 4
    for bit, block_ref in enumerate((hub0_ref, hub1_ref, hub2_ref, hub3_ref)):
        row = pl.multiple_of((here ^ bit) * 2 * HUB_DEV, 2 * HUB_DEV)
        hub_ref[pl.ds(row, 2 * HUB_DEV), :] = block_ref[...]
    bnd = bnd_ref[...].reshape(HALO, D)
    gself = jnp.zeros((D, D), F32)
    gnbr = jnp.zeros((D, D), F32)
    for i in range(ROWS // CHUNK):
        rows = slice(i * CHUNK, (i + 1) * CHUNK)
        agg = (
            part_ref[rows, :]
            + dot(rem_ref[rows, :HALO], bnd)
            + dot(rem_ref[rows, HALO:], hub_ref[...])
        ).astype(BF16)
        pre = self_ref[rows, :] + dot(agg, wn_ref[...])
        sig = jax.nn.sigmoid(pre)
        act_ref[rows, :] = (pre * sig).astype(BF16)
        pg = (cot_ref[rows, :].astype(F32) * sig * (1.0 + pre * (1.0 - sig))).astype(BF16)
        pg_ref[rows, :] = pg
        ag_ref[rows, :] = dot(pg, wnt_ref[...]).astype(BF16)
        gself = gself + dot(xt_ref[:, rows], pg)
        gnbr = gnbr + lax.dot_general(agg, pg, (((0,), (0,)), ((), ())), preferred_element_type=F32)
    bg_ref[...] = dot(atrem_ref[:HALO, :], ag_ref[...]).astype(BF16)
    hub_grad = dot(atrem_ref[HALO:, :], ag_ref[...])
    for k in range(8):
        lanes = slice(k // 4 * HALF, (k // 4 + 1) * HALF)
        rows = slice(k % 2 * PART, (k % 2 + 1) * PART)
        at = k * LOAD
        load_ref[at : at + PART, :] = (gself, gnbr)[k // 2 % 2][rows, lanes] * scale
        hub = hub_grad[k * HUB_DEV : (k + 1) * HUB_DEV, :]
        load_ref[at + PART : at + PART + HUB_DEV, :] = hub[:, :HALF]
        load_ref[at + PART + HUB_DEV : at + LOAD, :] = hub[:, HALF:]


def near_kernel(in_ref, bg_ref, out_ref, hub_ref):
    total = in_ref[:LOAD, :]
    for k in range(1, 8):
        total = total + in_ref[k * LOAD : (k + 1) * LOAD, :]
    hub_ref[:, :HALF] = total[PART : PART + HUB_DEV, :]
    hub_ref[:, HALF:] = total[PART + HUB_DEV :, :]
    out_ref[:, :D] = bg_ref[...]
    for m in range(NEAR):
        out_ref[m * 16 : (m + 1) * 16, D:] = halves(total[m * 8 : (m + 1) * 8, :])


def far_kernel(in_ref, out_ref):
    total = in_ref[:16, D:].astype(F32)
    for m in range(1, NEAR):
        total = total + in_ref[m * 16 : (m + 1) * 16, D:].astype(F32)
    chunk = total[:8, :] + total[8:, :]
    high = chunk.astype(BF16).astype(F32)
    both = jnp.concatenate([high, chunk - high], axis=1)
    moved = dot(permute(NEAR, ZH, ZH // 2), in_ref[:, :D])
    for j in range(ZH // 2):
        block = [moved[j * 64 : j * 64 + 32, :], both, moved[j * 64 + 32 : j * 64 + 64, :], both]
        out_ref[j * 2 * FAR : (j + 1) * 2 * FAR, :] = jnp.concatenate(block, axis=0).astype(BF16)


def far_blocks(in_ref):
    for j in range(ZH // 2):
        block = in_ref[j * 2 * FAR : (j + 1) * 2 * FAR, :].astype(F32)
        yield block[:FAR, :]
        yield block[FAR:, :]


def spread_kernel(in_ref, out_ref):
    total = jnp.zeros((8, D), F32)
    for block in far_blocks(in_ref):
        total = total + block[32:, :]
    chunk = total[:, :HALF] + total[:, HALF:]
    both = jnp.concatenate([chunk, chunk], axis=0).astype(BF16)
    for q in range(out_ref.shape[0] // 16):
        out_ref[q * 16 : (q + 1) * 16, :] = both


def final_kernel(
    count_ref, dst_ref, src_ref, send_ref, hub_ref, ret_ref, hsum_ref, pg_ref, ag_ref, ws_ref, tiles_ref,
    out_ref, at_ref,
):
    at_ref[...] = jnp.zeros_like(at_ref)

    def place(t, carry):
        source = src_ref[0, t]

        @pl.when(source < LOCAL)
        def _():
            row = pl.multiple_of(source * TILE, TILE)
            col = pl.multiple_of(dst_ref[0, t] * TILE, TILE)
            at_ref[pl.ds(row, TILE), pl.ds(col, TILE)] = tiles_ref[0, t].T

        return carry

    lax.fori_loop(0, count_ref[0], place, 0)
    blocks = [block[:32, :] for block in far_blocks(ret_ref)]
    ret = jnp.concatenate(blocks[ZH // 2 :] + blocks[: ZH // 2], axis=0).astype(BF16)
    high = hsum_ref[...].astype(BF16)
    low = (hsum_ref[...] - high.astype(F32)).astype(BF16)
    wst = ws_ref[...].T
    for i in range(ROWS // CHUNK):
        rows = slice(i * CHUNK, (i + 1) * CHUNK)
        total = dot(pg_ref[rows, :], wst) + dot(at_ref[rows, :], ag_ref[...])
        own = lax.broadcasted_iota(jnp.int32, (CHUNK, HALO), 0) + i * CHUNK
        total = total + dot(jnp.where(own == send_ref[...], 1.0, 0.0).astype(BF16), ret)
        own = lax.broadcasted_iota(jnp.int32, (CHUNK, HUB_DEV), 0) + i * CHUNK
        hub_hot = jnp.where(own == hub_ref[...], 1.0, 0.0).astype(BF16)
        total = total + dot(hub_hot, high) + dot(hub_hot, low)
        out_ref[rows, :] = total.astype(BF16)


def per_device(
    features, cotangent, w_self, w_nbr, tile_vals, tile_dst, tile_src, tile_count, send_rows, hub_rows
):
    mib = 1 << 20
    sent, hubs = call(
        pick_kernel, [((HALO // 2, 2, D), BF16), ((HUB_DEV, D), BF16)], [VM] * 3, flops=1 << 28, nbytes=mib
    )(send_rows, hub_rows, features)
    boundary = swap_rows(sent, (0, 1, 2), ZH // 2)
    hubs = lax.all_gather(hubs, "d", axis_index_groups=groups((4,)), axis=0, tiled=True)
    hub_blocks = [hubs]
    for bit in (1, 2, 3):
        hub_blocks.append(lax.ppermute(hubs, "d", [(i, i ^ (2 * bit)) for i in range(ALONG.size)]))
    rem, at_rem, part, self_pre, xt, wnt = call(
        prep_kernel,
        [
            ((ROWS, HALO + HUBS), BF16),
            ((HALO + HUBS, ROWS), BF16),
            ((ROWS, D), F32),
            ((ROWS, D), F32),
            ((D, ROWS), BF16),
            ((D, D), BF16),
        ],
        [SM, SM, SM, VM, VM, VM, VM],
        scratch=[pltpu.VMEM((ROWS, SOURCE * TILE), BF16), pltpu.VMEM((HALO + HUBS, ROWS), BF16)],
        flops=1 << 30,
        nbytes=9 * mib,
    )(tile_count, tile_dst, tile_src, tile_vals, features, w_self, w_nbr)
    act, pg, ag, bg, load = call(
        middle_kernel,
        [
            ((ROWS, D), BF16),
            ((ROWS, D), BF16),
            ((ROWS, D), BF16),
            ((HALO, D), BF16),
            ((8 * LOAD, HALF), F32),
        ],
        [VM] * 13,
        scratch=[pltpu.VMEM((HUBS, D), BF16)],
        flops=1 << 30,
        nbytes=8 * mib,
        trans=1 << 19,
    )(rem, at_rem, boundary, *hub_blocks, part, self_pre, cotangent, xt, w_nbr, wnt)

    load = swap_rows(load, (3, 4))
    near, hub_sums = call(
        near_kernel, [((HALO, PACK), BF16), ((HUB_DEV, D), F32)], [VM] * 2, nbytes=mib, limit=SMALL_LIMIT
    )(load, bg)
    near = swap_rows(near, (1, 2))
    (far,) = call(far_kernel, [((ZH * FAR, D), BF16)], [VM], nbytes=mib, limit=SMALL_LIMIT)(near)
    returned = swap_rows(far, (0,), ZH // 2)
    (chunk,) = call(spread_kernel, [((4 * D, HALF), BF16)], [VM], nbytes=mib, limit=SMALL_LIMIT)(returned)
    grads = swap_rows(chunk, (3, 4, 1, 2))
    (grad_features,) = call(
        final_kernel,
        [((ROWS, D), BF16)],
        [SM] * 3 + [VM] * 8,
        scratch=[pltpu.VMEM((ROWS, ROWS), BF16)],
        flops=1 << 30,
        nbytes=5 * mib,
    )(tile_count, tile_dst, tile_src, send_rows, hub_rows, returned, hub_sums, pg, ag, w_self, tile_vals)
    grads = grads.astype(F32).reshape(2, 2, D, HALF)
    grads = jnp.concatenate([grads[0], grads[1]], axis=2)
    return act, grad_features, grads[0], grads[1]


def solution(mesh):
    whole = P("d", None)
    return jax.shard_map(
        per_device,
        mesh=Mesh(mesh.devices.reshape(-1), ("d",)),
        in_specs=(
            whole,
            whole,
            P(),
            P(),
            P("d", None, None, None),
            whole,
            whole,
            P("d"),
            whole,
            whole,
        ),
        out_specs=(whole, whole, P(), P()),
        check_vma=False,
    )
```
